512 devices in a mesh: ctx: 32 (over z, y_hi, core), tp: 16 (over x, y_lo).
Axes of the slice: x: 4, y: 8 (y_hi: 2, y_lo: 4; y = y_hi * 4 + y_lo), z: 8, core: 2. Of those that a mesh axis runs over, the one named last changes fastest.
Arguments:
- q_proj: bfloat16 [4096, 4096], P('ctx', 'tp'), may hold values from -6 to 6
- k_proj: bfloat16 [4096, 4096], P('ctx', 'tp'), may hold values from -6 to 6
- v_proj: bfloat16 [4096, 4096], P('ctx', 'tp'), may hold values from -6 to 6
- saved_conv: bfloat16 [4096, 4096], P('ctx', 'tp'), may hold values from -6 to 6
- out_grad: bfloat16 [4096, 4096], P('ctx', 'tp'), may hold values from -6 to 6
- out_weight: bfloat16 [4096, 4096], P('tp'), may hold values from -0.09375 to 0.09375
- filter_taps: bfloat16 [4096, 4096], P('ctx', 'tp'), may hold values from -1.1 to 1.1
Outputs:
- dq_grad: bfloat16 [4096, 4096], P('ctx', 'tp')
- dk_grad: bfloat16 [4096, 4096], P('ctx', 'tp')
- dv_grad: bfloat16 [4096, 4096], P('ctx', 'tp')
- filter_grad: float32 [4096, 4096], P('ctx', 'tp')
The draws below stay inside these ranges and needn't reach their ends.
All inputs are finite; a program needn't handle non-finite values.
Results may differ from the reference program's by a relative error of at most 0.003.
Values may be sent and summed in bfloat16 or wider, within the bound.
A program may use at most 128 MiB of HBM per device.

```python
import math
import jax
import jax.numpy as jnp

D = 4096
SEQ = 4096


def draw_filter_taps(key, part):
    first, second = jax.random.split(jax.random.fold_in(key, 7))
    noise = jnp.clip(jax.random.normal(first, (SEQ, D), jnp.float32), -4.0, 4.0)
    log_rate = jax.random.uniform(second, (1, D), jnp.float32, math.log(0.5 / SEQ), math.log(1.0 / 30.0))
    rate = jnp.exp(log_rate)
    lags = jnp.arange(SEQ, dtype=jnp.float32)[:, None]
    scale = jnp.sqrt((1.0 - jnp.exp(-2.0 * rate)) / (1.0 - jnp.exp(-2.0 * rate * SEQ)))
    return (noise * scale * jnp.exp(-rate * lags)).astype(jnp.bfloat16)


def block_scale(rng, shape, cuts, smallest, largest):
    factor_of = 1.0
    for position, shards_of in cuts:
        heights = jax.random.uniform(jax.random.fold_in(jax.random.fold_in(rng, 6), position), (shards_of,), jnp.float32, smallest / len(cuts), largest / len(cuts))
        factor_of = factor_of * jnp.repeat(jnp.exp(heights), shape[position] // shards_of).reshape((-1,) + (1,) * (len(shape) - 1 - position))
    return factor_of


def centred(rng, extent, scale, limit, cuts=(), kind=jnp.bfloat16):
    entries = scale * jax.random.normal(rng, extent, jnp.float32)
    if cuts:
        entries = entries * block_scale(rng, extent, cuts, -0.22, 0.18)
    return jnp.clip(entries, -limit, limit).astype(kind)


def setup_inputs(seed: int = 0) -> dict:
    key_list = jax.random.split(jax.random.key(seed), 8)
    return {
        "q_proj": centred(key_list[0], (SEQ, D), 1.0, 6.0, ((0, 32), (1, 16))),
        "k_proj": centred(key_list[1], (SEQ, D), 1.0, 6.0, ((0, 32), (1, 16))),
        "v_proj": centred(key_list[2], (SEQ, D), 1.0, 6.0, ((0, 32), (1, 16))),
        "saved_conv": centred(key_list[3], (SEQ, D), 1.0, 6.0, ((0, 32), (1, 16))),
        "out_grad": centred(key_list[4], (SEQ, D), 1.0, 6.0, ((0, 32), (1, 16))),
        "out_weight": centred(key_list[5], (D, D), D ** -0.5, 0.09375, ((0, 16),)),
        "filter_taps": draw_filter_taps(jax.random.fold_in(key_list[7], 71), 0),
    }


def reference(q_proj, k_proj, v_proj, saved_conv, out_grad, out_weight, filter_taps):
    d_gated = jnp.dot(out_grad, out_weight.T, preferred_element_type=jnp.float32)
    dq_grad = (d_gated * saved_conv.astype(jnp.float32)).astype(jnp.bfloat16)
    dz = d_gated * q_proj.astype(jnp.float32)
    gated = (k_proj.astype(jnp.float32) * v_proj.astype(jnp.float32)).astype(jnp.bfloat16)
    length = 2 * SEQ
    dz_spec = jnp.fft.rfft(dz, n=length, axis=0)
    filter_spec = jnp.fft.rfft(filter_taps.astype(jnp.float32), n=length, axis=0)
    du = jnp.fft.irfft(jnp.conj(filter_spec) * dz_spec, n=length, axis=0)[:SEQ].astype(jnp.float32)
    gated_spec = jnp.fft.rfft(gated.astype(jnp.float32), n=length, axis=0)
    lagged = jnp.fft.irfft(jnp.conj(gated_spec) * dz_spec, n=length, axis=0)[:SEQ].astype(jnp.float32)
    filter_grad = lagged * (float(SEQ) ** -0.5)
    dk_grad = (du * v_proj.astype(jnp.float32)).astype(jnp.bfloat16)
    dv_grad = (du * k_proj.astype(jnp.float32)).astype(jnp.bfloat16)
    return dq_grad, dk_grad, dv_grad, filter_grad.astype(jnp.float32)
```

```python
import functools
import math

import jax
import jax.numpy as jnp
import ml_dtypes
import numpy as np
from jax import lax
from jax.experimental import pallas as pl
from jax.experimental.pallas import tpu as pltpu
from jax.sharding import PartitionSpec as P

MESH = pl.DeviceIdType.MESH
F32 = jnp.float32
BF16 = jnp.bfloat16
XN = 4
YN = 4
GROUP = 8


def halves(table):
    upper = table.astype(ml_dtypes.bfloat16)
    lower = (table - upper.astype(np.float64)).astype(ml_dtypes.bfloat16)
    return np.concatenate([upper, lower], axis=1)


def make_tables(block):
    n = np.arange(block)
    turns = np.outer(n, 2 * n + 1) % (4 * block)
    angle = turns * (math.pi / (2 * block))
    forward = np.concatenate([np.cos(angle), -np.sin(angle)], axis=1)
    back = np.concatenate([np.cos(angle).T, -np.sin(angle).T], axis=0) / block
    return halves(forward), halves(back)


def split(value):
    upper = value.astype(BF16)
    return upper, (value - upper.astype(F32)).astype(BF16)


def mm(left, right):
    return jnp.dot(left, right, preferred_element_type=F32)


def fused(
    nctx, f_hbm, k_hbm, v_hbm, q_hbm, og_hbm, s_hbm, w_hbm, fwd_hbm, inv_hbm,
    dq_ref, dk_ref, dv_ref, fg_ref,
    f_ref, k_ref, v_ref, q_ref, og_ref, s_ref, w, fwd, inv, og_all, acc, qt, fgs, xf, zs, zin, xspec, zt, obuf, rs, ret,
    local_sem, send_ag, recv_y, recv_x, recv_r, send_f, recv_f, send_z, recv_z, send_o, recv_o,
):
    rows, chans = q_ref.shape
    nb = nctx // 2
    block = 2 * rows
    half = rows // 2
    me_c = lax.axis_index("ctx")
    me_t = lax.axis_index("tp")
    x = lax.div(me_t, YN)
    y = lax.rem(me_t, YN)
    right = lax.rem(x + 1, XN)
    left = lax.rem(x + XN - 1, XN)
    across = lax.rem(x + 2, XN)
    line = [y, y + 1 - 2 * lax.rem(y, 2), lax.rem(y + 2, YN), YN - 1 - y]
    slot_me = lax.rem(me_c, 2) * nb + lax.div(me_c, 2)

    sources = (og_hbm, f_hbm, k_hbm, v_hbm, q_hbm, w_hbm, s_hbm, fwd_hbm, inv_hbm)
    targets = (og_ref, f_ref, k_ref, v_ref, q_ref, w, s_ref, fwd, inv)
    loads = [
        pltpu.make_async_copy(source, target, local_sem.at[i])
        for i, (source, target) in enumerate(zip(sources, targets))
    ]
    for load in loads:
        load.start()

    barrier = pltpu.get_barrier_semaphore()

    def signal(c, t):
        pl.semaphore_signal(barrier, inc=1, device_id=(c, t), device_id_type=MESH)

    signal(me_c, right * YN + y)
    signal(me_c, left * YN + y)
    for j in range(1, YN):
        signal(me_c, x * YN + line[j])

    @pl.loop(1, nctx)
    def _(i):
        signal(lax.rem(me_c + i, nctx), me_t)

    for load in loads[:5]:
        load.wait()
    ft = f_ref[...].astype(F32).T.reshape(nctx, GROUP, rows)
    gated = (k_ref[...].astype(F32) * v_ref[...].astype(F32)).astype(BF16)
    gt = gated.astype(F32).T.reshape(nctx, GROUP, rows)
    fgs[...] = jnp.concatenate([ft, gt], axis=1).astype(BF16)
    qt[...] = q_ref[...].astype(F32).T
    xf[slot_me] = fgs[me_c]

    pl.semaphore_wait(barrier, nctx - 1 + YN + 1)

    def part(ref, h):
        return ref.at[pl.ds(h * half, half), :]

    def send(src, slot, h, dest_x, dest_y, sem):
        pltpu.make_async_remote_copy(
            src_ref=src,
            dst_ref=og_all.at[slot, pl.ds(h * half, half), :],
            send_sem=send_ag,
            recv_sem=sem,
            device_id=(me_c, dest_x * YN + dest_y),
            device_id_type=MESH,
        ).start()

    def arrived(slot, h, sem):
        dst = og_all.at[slot, pl.ds(h * half, half), :]
        pltpu.make_async_copy(dst, dst, sem).wait()

    def send_x(j):
        slot = x * YN + line[j]
        for h in range(2):
            for way, dest in ((h, right if h == 0 else left), (1 - h, left if h == 0 else right)):
                src = part(og_ref, h) if j == 0 else og_all.at[slot, pl.ds(h * half, half), :]
                send(src, slot, h, dest, y, recv_x.at[way, j, h])

    def relay(j):
        for h, source, dest in ((0, left, right), (1, right, left)):
            slot = source * YN + line[j]
            arrived(slot, h, recv_x.at[h, j, h])
            send(og_all.at[slot, pl.ds(h * half, half), :], slot, h, dest, y, recv_r.at[j, h])

    def add(slot, block_value):
        cols = pl.ds(pl.multiple_of(slot * chans, chans), chans)
        acc[...] += lax.dot_general(
            w[:, cols], block_value, (((1,), (1,)), ((), ())), preferred_element_type=F32
        )

    def add_near(j):
        for way, source in ((0, left), (1, right)):
            slot = source * YN + line[j]
            arrived(slot, 1 - way, recv_x.at[way, j, 1 - way])
            add(slot, og_all[slot])

    def add_far(j):
        slot = across * YN + line[j]
        for h in range(2):
            arrived(slot, h, recv_r.at[j, h])
        add(slot, og_all[slot])

    def forward_line(j):
        slot = x * YN + line[j]
        for h in range(2):
            arrived(slot, h, recv_y.at[j - 1, h])
        send_x(j)

    send_x(0)
    for j in range(1, YN):
        for h in range(2):
            send(part(og_ref, h), me_t, h, x, line[j], recv_y.at[j - 1, h])

    def exchange(src, dst, send_sem, recv_sem):
        @pl.loop(1, nctx)
        def _(i):
            peer = lax.rem(me_c + i, nctx)
            pltpu.make_async_remote_copy(
                src_ref=src(peer),
                dst_ref=dst,
                send_sem=send_sem,
                recv_sem=recv_sem,
                device_id=(peer, me_t),
                device_id_type=MESH,
            ).start()

    def drain(ref, count, sem):
        whole = ref.at[pl.ds(0, count)]
        pltpu.make_async_copy(whole, whole, sem).wait()

    exchange(lambda p: fgs.at[p], xf.at[slot_me], send_f, recv_f)

    for load in loads[5:]:
        load.wait()
    acc[...] = lax.dot_general(
        w[:, pl.ds(pl.multiple_of(me_t * chans, chans), chans)], og_ref[...],
        (((1,), (1,)), ((), ())), preferred_element_type=F32,
    )
    for j in range(1, YN):
        forward_line(j)
        relay(j - 1)
        slot = x * YN + line[j]
        add(slot, og_all[slot])
        add_near(j - 1)
        if j >= 2:
            add_far(j - 2)
    relay(YN - 1)
    add_near(YN - 1)
    add_far(YN - 2)
    add_far(YN - 1)

    zs[...] = (acc[...] * qt[...]).reshape(nctx, GROUP, rows)
    exchange(lambda p: zs.at[p], zin.at[slot_me], send_z, recv_z)
    zin[slot_me] = zs[me_c]

    dq_ref[...] = (acc[...].T * s_ref[...].astype(F32)).astype(BF16)
    drain(xf, nctx - 1, recv_f)
    taps = jnp.concatenate(
        [
            xf[pl.ds(0, nb)].reshape(nb * 2 * GROUP, rows),
            xf[pl.ds(nb, nb)].reshape(nb * 2 * GROUP, rows),
        ],
        axis=1,
    )
    both = mm(taps, fwd[...])
    xspec[...] = (both[:, : 2 * block] + both[:, 2 * block :]).reshape(nb, 2 * GROUP, 2 * block)
    lane = lax.broadcasted_iota(jnp.int32, (1, 1, block), 2)
    sign = (1 - 2 * lax.rem(lane, 2)).astype(F32)

    drain(zin, nctx - 1, recv_z)
    signal_in = jnp.concatenate(
        [
            zin[pl.ds(0, nb)].reshape(nb * GROUP, rows),
            zin[pl.ds(nb, nb)].reshape(nb * GROUP, rows),
        ],
        axis=1,
    )
    upper, lower = split(signal_in)
    spec = mm(upper, fwd[...])
    spec = spec[:, : 2 * block] + spec[:, 2 * block :] + mm(lower, fwd[:, : 2 * block])
    spec = spec.reshape(nb, GROUP, 2 * block)
    real, imag = spec[:, :, :block], spec[:, :, block:]
    none = jnp.zeros((1, GROUP, block), F32)
    next_real = jnp.concatenate([real[1:], none], axis=0)
    next_imag = jnp.concatenate([imag[1:], none], axis=0)
    zt[pl.ds(0, nb), :, pl.ds(0, block)] = real + sign * next_imag
    zt[pl.ds(0, nb), :, pl.ds(block, block)] = imag - sign * next_real
    tile = min(4, nb)
    zt[pl.ds(nb, tile)] = jnp.zeros((tile, GROUP, 2 * block), F32)

    width = 128
    for part_of in range(block // width):
        re_cols = pl.ds(part_of * width, width)
        im_cols = pl.ds(block + part_of * width, width)
        for first in range(0, nb, tile):

            def steps(step, sums, re_cols=re_cols, im_cols=im_cols, first=first):
                sums = list(sums)
                for u in range(tile):
                    j = step * tile + u
                    taps_re = xspec[j, :, re_cols]
                    taps_im = xspec[j, :, im_cols]
                    for i in range(tile):
                        z_re = zt[j + first + i, :, re_cols]
                        z_im = zt[j + first + i, :, im_cols]
                        for kind in range(2):
                            a = taps_re[kind * GROUP : (kind + 1) * GROUP]
                            b = taps_im[kind * GROUP : (kind + 1) * GROUP]
                            at = (i * 2 + kind) * 2
                            sums[at] = sums[at] + (a * z_re + b * z_im)
                            sums[at + 1] = sums[at + 1] + (a * z_im - b * z_re)
                return tuple(sums)

            zero = jnp.zeros((GROUP, width), F32)
            sums = lax.fori_loop(0, (nb - first) // tile, steps, (zero,) * (4 * tile))
            for i in range(tile):
                for kind in range(2):
                    at = (i * 2 + kind) * 2
                    lines = pl.ds(kind * GROUP, GROUP)
                    obuf[first + i, lines, re_cols] = sums[at]
                    obuf[first + i, lines, im_cols] = sums[at + 1]

    upper, lower = split(obuf[...].reshape(nb * 2 * GROUP, 2 * block))
    both = mm(upper, inv[...])
    res = both[:, :block] + both[:, block:] + mm(lower, inv[:, :block])
    rs[pl.ds(0, nb)] = res[:, :rows].reshape(nb, 2 * GROUP, rows)
    rs[pl.ds(nb, nb)] = res[:, rows:].reshape(nb, 2 * GROUP, rows)
    exchange(
        lambda p: rs.at[lax.rem(p, 2) * nb + lax.div(p, 2)], ret.at[me_c], send_o, recv_o
    )
    ret[me_c] = rs[slot_me]

    drain(ret, nctx - 1, recv_o)
    du = ret[:, pl.ds(0, GROUP), :].reshape(chans, rows).T
    dk_ref[...] = (du * v_ref[...].astype(F32)).astype(BF16)
    dv_ref[...] = (du * k_ref[...].astype(F32)).astype(BF16)
    lagged = ret[:, pl.ds(GROUP, GROUP), :].reshape(chans, rows).T
    fg_ref[...] = lagged * float(rows * nctx) ** (-0.5)

    drain(og_all, XN * YN - 1, send_ag)
    drain(fgs, nctx - 1, send_f)
    drain(zs, nctx - 1, send_z)
    drain(rs, nctx - 1, send_o)


def body(q_proj, k_proj, v_proj, saved_conv, out_grad, out_weight, filter_taps):
    rows, chans = q_proj.shape
    nctx = lax.axis_size("ctx")
    nb = nctx // 2
    block = 2 * rows
    forward, back = make_tables(block)
    vmem = pl.BlockSpec(memory_space=pltpu.VMEM)
    anywhere = pl.BlockSpec(memory_space=pl.ANY)
    dma = pltpu.SemaphoreType.DMA
    narrow = jax.ShapeDtypeStruct((rows, chans), BF16)
    return pl.pallas_call(
        functools.partial(fused, nctx),
        out_shape=(narrow, narrow, narrow, jax.ShapeDtypeStruct((rows, chans), F32)),
        in_specs=[anywhere] * 9,
        out_specs=(vmem,) * 4,
        scratch_shapes=[pltpu.VMEM((rows, chans), BF16)] * 6
        + [
            pltpu.VMEM(out_weight.shape, BF16),
            pltpu.VMEM(forward.shape, BF16),
            pltpu.VMEM(back.shape, BF16),
            pltpu.VMEM((XN * YN, rows, chans), BF16),
            pltpu.VMEM((chans, rows), F32),
            pltpu.VMEM((chans, rows), F32),
            pltpu.VMEM((nctx, 2 * GROUP, rows), BF16),
            pltpu.VMEM((nctx, 2 * GROUP, rows), BF16),
            pltpu.VMEM((nctx, GROUP, rows), F32),
            pltpu.VMEM((nctx, GROUP, rows), F32),
            pltpu.VMEM((nb, 2 * GROUP, 2 * block), F32),
            pltpu.VMEM((nb + 4, GROUP, 2 * block), F32),
            pltpu.VMEM((nb, 2 * GROUP, 2 * block), F32),
            pltpu.VMEM((nctx, 2 * GROUP, rows), F32),
            pltpu.VMEM((nctx, 2 * GROUP, rows), F32),
            dma((9,)),
            dma,
            dma((YN - 1, 2)),
            dma((2, YN, 2)),
            dma((YN, 2)),
        ]
        + [dma] * 6,
        compiler_params=pltpu.CompilerParams(
            collective_id=0, has_side_effects=True, vmem_limit_bytes=63 * 1024 * 1024
        ),
    )(
        filter_taps, k_proj, v_proj, q_proj, out_grad, saved_conv, out_weight,
        jnp.asarray(forward), jnp.asarray(back),
    )


def solution(mesh):
    block = P("ctx", "tp")
    in_specs = (block, block, block, block, block, P("tp", None), block)
    return jax.shard_map(
        body, mesh=mesh, in_specs=in_specs, out_specs=(block,) * 4, check_vma=False
    )
```

```python
import functools
import math

import jax
import jax.numpy as jnp
import ml_dtypes
import numpy as np
from jax import lax
from jax.experimental import pallas as pl
from jax.experimental.pallas import tpu as pltpu
from jax.sharding import PartitionSpec as P

MESH = pl.DeviceIdType.MESH
F32 = jnp.float32
BF16 = jnp.bfloat16
XN = 4
YN = 4
GROUP = 8
DIRECT = (0, 3)


def halves(table):
    upper = table.astype(ml_dtypes.bfloat16)
    lower = (table - upper.astype(np.float64)).astype(ml_dtypes.bfloat16)
    return np.concatenate([upper, lower], axis=1)


def make_tables(block):
    n = np.arange(block)
    turns = np.outer(n, 2 * n + 1) % (4 * block)
    angle = turns * (math.pi / (2 * block))
    forward = np.concatenate([np.cos(angle), -np.sin(angle)], axis=1)
    back = np.concatenate([np.cos(angle).T, -np.sin(angle).T], axis=0) / block
    return halves(forward), halves(back)


def far_first(nctx):
    def hops(i):
        along = min(i // 4, nctx // 4 - i // 4)
        return along + (YN if (i // 2) % 2 else 0)

    return sorted(range(1, nctx), key=hops, reverse=True)


def split(value):
    upper = value.astype(BF16)
    return upper, (value - upper.astype(F32)).astype(BF16)


def mm(left, right):
    return jnp.dot(left, right, preferred_element_type=F32)


def fused(
    nctx, f_hbm, k_hbm, v_hbm, q_hbm, og_hbm, w_hbm, fwd_hbm, inv_hbm,
    ret, acc_hbm,
    f_ref, k_ref, v_ref, q_ref, og_ref, w, fwd, inv, og_all, acc, qt, fgs, xf, zs, zin, xspec, zt, obuf, rs,
    ready, local_sem, send_ag, recv_y, recv_x, recv_r, send_f, recv_f, send_z, recv_z, send_o, recv_o,
):
    rows, chans = q_ref.shape
    nb = nctx // 2
    block = 2 * rows
    half = rows // 2
    me_c = lax.axis_index("ctx")
    me_t = lax.axis_index("tp")
    x = lax.div(me_t, YN)
    y = lax.rem(me_t, YN)
    right = lax.rem(x + 1, XN)
    left = lax.rem(x + XN - 1, XN)
    across = lax.rem(x + 2, XN)
    line = [y, y + 1 - 2 * lax.rem(y, 2), lax.rem(y + 2, YN), YN - 1 - y]
    slot_me = lax.rem(me_c, 2) * nb + lax.div(me_c, 2)

    sources = (og_hbm, f_hbm, k_hbm, v_hbm, q_hbm, w_hbm, fwd_hbm, inv_hbm)
    targets = (og_ref, f_ref, k_ref, v_ref, q_ref, w, fwd, inv)
    loads = [
        pltpu.make_async_copy(source, target, local_sem.at[i])
        for i, (source, target) in enumerate(zip(sources, targets))
    ]
    for load in loads:
        load.start()

    barrier = pltpu.get_barrier_semaphore()

    def signal(c, t):
        pl.semaphore_signal(barrier, inc=1, device_id=(c, t), device_id_type=MESH)

    core = me_c + 1 - 2 * lax.rem(me_c, 2)
    turn = 2 - 4 * lax.rem(lax.div(me_c, 2), 2)
    chip_set = (core, me_c + turn, core + turn)

    def around(steps):
        return [lax.rem(me_c + i, nctx) for i in sorted({steps % nctx, -steps % nctx} - {0})]

    for t in (right, left, across):
        signal(me_c, t * YN + y)
    for j in range(1, YN):
        signal(me_c, x * YN + line[j])
    near = (*around(4), *chip_set)
    for c in near:
        signal(c, me_t)

    def tell(partners, sem):
        for c in partners:
            pl.semaphore_signal(sem, inc=1, device_id=(c, me_t), device_id_type=MESH)

    loads[0].wait()
    pl.semaphore_wait(barrier, 3 + YN - 1 + len(near))
    tell(chip_set, ready.at[0])

    def part(ref, h):
        return ref.at[pl.ds(h * half, half), :]

    def send(src, slot, h, dest_x, dest_y, sem):
        pltpu.make_async_remote_copy(
            src_ref=src,
            dst_ref=og_all.at[slot, pl.ds(h * half, half), :],
            send_sem=send_ag,
            recv_sem=sem,
            device_id=(me_c, dest_x * YN + dest_y),
            device_id_type=MESH,
        ).start()

    def arrived(slot, h, sem):
        dst = og_all.at[slot, pl.ds(h * half, half), :]
        pltpu.make_async_copy(dst, dst, sem).wait()

    def send_x(j, h):
        slot = x * YN + line[j]
        src = part(og_ref, h) if j == 0 else og_all.at[slot, pl.ds(h * half, half), :]
        if j in DIRECT:
            send(src, slot, h, across, y, recv_r.at[j, h])
        first, second = (right, left) if h == 0 else (left, right)
        send(src, slot, h, first, y, recv_x.at[h, j, h])
        send(src, slot, h, second, y, recv_x.at[1 - h, j, h])

    def relay(j):
        for h, source, dest in ((0, left, right), (1, right, left)):
            slot = source * YN + line[j]
            arrived(slot, h, recv_x.at[h, j, h])
            if j in DIRECT:
                continue
            send(og_all.at[slot, pl.ds(h * half, half), :], slot, h, dest, y, recv_r.at[j, h])

    def add(slot, block_value):
        cols = pl.ds(pl.multiple_of(slot * chans, chans), chans)
        acc[...] += lax.dot_general(
            w[:, cols], block_value, (((1,), (1,)), ((), ())), preferred_element_type=F32
        )

    def add_near(j):
        for way, source in ((0, left), (1, right)):
            slot = source * YN + line[j]
            arrived(slot, 1 - way, recv_x.at[way, j, 1 - way])
            add(slot, og_all[slot])

    def add_far(j):
        slot = across * YN + line[j]
        for h in range(2):
            arrived(slot, h, recv_r.at[j, h])
        add(slot, og_all[slot])

    def forward_line(j):
        slot = x * YN + line[j]
        for h in range(2):
            arrived(slot, h, recv_y.at[j - 1, h])
            send_x(j, h)

    for h in range(2):
        for j in range(1, YN):
            send(part(og_ref, h), me_t, h, x, line[j], recv_y.at[j - 1, h])
        send_x(0, h)

    def exchange(src, dst, send_sem, recv_sem):
        for i in far_first(nctx):
            peer = lax.rem(me_c + i, nctx)
            pltpu.make_async_remote_copy(
                src_ref=src(peer),
                dst_ref=dst,
                send_sem=send_sem,
                recv_sem=recv_sem,
                device_id=(peer, me_t),
                device_id_type=MESH,
            ).start()

    def drain(ref, count, sem):
        whole = ref.at[pl.ds(0, count)]
        pltpu.make_async_copy(whole, whole, sem).wait()

    for load in loads[1:5]:
        load.wait()
    ft = f_ref[...].astype(F32).T.reshape(nctx, GROUP, rows)
    gated = (k_ref[...].astype(F32) * v_ref[...].astype(F32)).astype(BF16)
    gt = gated.astype(F32).T.reshape(nctx, GROUP, rows)
    fgs[...] = jnp.concatenate([ft, gt], axis=1).astype(BF16)
    qt[...] = q_ref[...].astype(F32).T
    xf[slot_me] = fgs[me_c]

    for load in loads[5:]:
        load.wait()
    acc[...] = lax.dot_general(
        w[:, pl.ds(pl.multiple_of(me_t * chans, chans), chans)], og_ref[...],
        (((1,), (1,)), ((), ())), preferred_element_type=F32,
    )
    rounds = (chip_set, around(4), around(8))
    for j in range(1, YN):
        forward_line(j)
        relay(j - 1)
        pl.semaphore_wait(ready.at[j - 1], len(rounds[j - 1]))
        if j < 3:
            tell(rounds[j], ready.at[j])
        else:
            exchange(lambda p: fgs.at[p], xf.at[slot_me], send_f, recv_f)
        slot = x * YN + line[j]
        add(slot, og_all[slot])
        add_near(j - 1)
        if j >= 2:
            add_far(j - 2)
    relay(YN - 1)
    add_near(YN - 1)
    add_far(YN - 2)
    add_far(YN - 1)

    zs[...] = (acc[...] * qt[...]).reshape(nctx, GROUP, rows)
    exchange(lambda p: zs.at[p], zin.at[slot_me], send_z, recv_z)
    zin[slot_me] = zs[me_c]

    save = pltpu.make_async_copy(acc, acc_hbm, local_sem.at[8])
    save.start()
    drain(xf, nctx - 1, recv_f)
    taps = jnp.concatenate(
        [
            xf[pl.ds(0, nb)].reshape(nb * 2 * GROUP, rows),
            xf[pl.ds(nb, nb)].reshape(nb * 2 * GROUP, rows),
        ],
        axis=1,
    )
    both = mm(taps, fwd[...])
    xspec[...] = (both[:, : 2 * block] + both[:, 2 * block :]).reshape(nb, 2 * GROUP, 2 * block)
    lane = lax.broadcasted_iota(jnp.int32, (1, 1, block), 2)
    sign = (1 - 2 * lax.rem(lane, 2)).astype(F32)

    drain(zin, nctx - 1, recv_z)
    signal_in = jnp.concatenate(
        [
            zin[pl.ds(0, nb)].reshape(nb * GROUP, rows),
            zin[pl.ds(nb, nb)].reshape(nb * GROUP, rows),
        ],
        axis=1,
    )
    upper, lower = split(signal_in)
    spec = mm(upper, fwd[...])
    spec = spec[:, : 2 * block] + spec[:, 2 * block :] + mm(lower, fwd[:, : 2 * block])
    spec = spec.reshape(nb, GROUP, 2 * block)
    real, imag = spec[:, :, :block], spec[:, :, block:]
    none = jnp.zeros((1, GROUP, block), F32)
    next_real = jnp.concatenate([real[1:], none], axis=0)
    next_imag = jnp.concatenate([imag[1:], none], axis=0)
    zt[pl.ds(0, nb), :, pl.ds(0, block)] = real + sign * next_imag
    zt[pl.ds(0, nb), :, pl.ds(block, block)] = imag - sign * next_real
    tile = min(4, nb)
    zt[pl.ds(nb, tile)] = jnp.zeros((tile, GROUP, 2 * block), F32)

    width = 128
    for part_of in range(block // width):
        re_cols = pl.ds(part_of * width, width)
        im_cols = pl.ds(block + part_of * width, width)
        for first in range(0, nb, tile):

            def steps(step, sums, re_cols=re_cols, im_cols=im_cols, first=first):
                sums = list(sums)
                for u in range(tile):
                    j = step * tile + u
                    taps_re = xspec[j, :, re_cols]
                    taps_im = xspec[j, :, im_cols]
                    for i in range(tile):
                        z_re = zt[j + first + i, :, re_cols]
                        z_im = zt[j + first + i, :, im_cols]
                        for kind in range(2):
                            a = taps_re[kind * GROUP : (kind + 1) * GROUP]
                            b = taps_im[kind * GROUP : (kind + 1) * GROUP]
                            at = (i * 2 + kind) * 2
                            sums[at] = sums[at] + (a * z_re + b * z_im)
                            sums[at + 1] = sums[at + 1] + (a * z_im - b * z_re)
                return tuple(sums)

            zero = jnp.zeros((GROUP, width), F32)
            sums = lax.fori_loop(0, (nb - first) // tile, steps, (zero,) * (4 * tile))
            for i in range(tile):
                for kind in range(2):
                    at = (i * 2 + kind) * 2
                    lines = pl.ds(kind * GROUP, GROUP)
                    obuf[first + i, lines, re_cols] = sums[at]
                    obuf[first + i, lines, im_cols] = sums[at + 1]

    upper, lower = split(obuf[...].reshape(nb * 2 * GROUP, 2 * block))
    both = mm(upper, inv[...])
    res = both[:, :block] + both[:, block:] + mm(lower, inv[:, :block])
    rs[pl.ds(0, nb)] = res[:, :rows].reshape(nb, 2 * GROUP, rows)
    rs[pl.ds(nb, nb)] = res[:, rows:].reshape(nb, 2 * GROUP, rows)
    exchange(
        lambda p: rs.at[lax.rem(p, 2) * nb + lax.div(p, 2)], ret.at[me_c], send_o, recv_o
    )
    own = pltpu.make_async_copy(rs.at[slot_me], ret.at[me_c], local_sem.at[9])
    own.start()
    drain(ret, nctx - 1, recv_o)
    own.wait()
    save.wait()
    drain(og_all, XN * YN - 1, send_ag)
    drain(fgs, nctx - 1, send_f)
    drain(zs, nctx - 1, send_z)
    drain(rs, nctx - 1, send_o)


def finish(
    ret_hbm, acc_hbm, s_hbm, k_hbm, v_hbm, dq_hbm, dk_hbm, dv_hbm, fg_hbm,
    ret, acc, s_ref, k_ref, v_ref, dq, dk, dv, fg, sem_in, sem_out,
):
    rows, chans = s_ref.shape
    loads = [
        pltpu.make_async_copy(source, target, sem_in.at[i])
        for i, (source, target) in enumerate(
            ((acc_hbm, acc), (s_hbm, s_ref), (ret_hbm, ret), (k_hbm, k_ref), (v_hbm, v_ref))
        )
    ]
    for load in loads:
        load.start()
    stores = [
        pltpu.make_async_copy(source, target, sem_out.at[i])
        for i, (source, target) in enumerate(
            ((dq, dq_hbm), (dk, dk_hbm), (dv, dv_hbm), (fg, fg_hbm))
        )
    ]
    loads[0].wait()
    loads[1].wait()
    dq[...] = (acc[...].T * s_ref[...].astype(F32)).astype(BF16)
    stores[0].start()
    loads[2].wait()
    lagged = ret[:, pl.ds(GROUP, GROUP), :].reshape(chans, rows).T
    fg[...] = lagged * float(rows * ret.shape[0]) ** (-0.5)
    stores[3].start()
    du = ret[:, pl.ds(0, GROUP), :].reshape(chans, rows).T
    loads[3].wait()
    loads[4].wait()
    dk[...] = (du * v_ref[...].astype(F32)).astype(BF16)
    stores[1].start()
    dv[...] = (du * k_ref[...].astype(F32)).astype(BF16)
    stores[2].start()
    for store in stores:
        store.wait()


def body(q_proj, k_proj, v_proj, saved_conv, out_grad, out_weight, filter_taps):
    rows, chans = q_proj.shape
    nctx = lax.axis_size("ctx")
    nb = nctx // 2
    block = 2 * rows
    forward, back = make_tables(block)
    hbm = pl.BlockSpec(memory_space=pltpu.HBM)
    dma = pltpu.SemaphoreType.DMA
    narrow = jax.ShapeDtypeStruct((rows, chans), BF16)
    shapes = (narrow, narrow, narrow, jax.ShapeDtypeStruct((rows, chans), F32))
    results = pl.pallas_call(
        functools.partial(fused, nctx),
        out_shape=(
            jax.ShapeDtypeStruct((nctx, 2 * GROUP, rows), F32),
            jax.ShapeDtypeStruct((chans, rows), F32),
        ),
        in_specs=[hbm] * 8,
        out_specs=(hbm,) * 2,
        scratch_shapes=[pltpu.VMEM((rows, chans), BF16)] * 5
        + [
            pltpu.VMEM(out_weight.shape, BF16),
            pltpu.VMEM(forward.shape, BF16),
            pltpu.VMEM(back.shape, BF16),
            pltpu.VMEM((XN * YN, rows, chans), BF16),
            pltpu.VMEM((chans, rows), F32),
            pltpu.VMEM((chans, rows), F32),
            pltpu.VMEM((nctx, 2 * GROUP, rows), BF16),
            pltpu.VMEM((nctx, 2 * GROUP, rows), BF16),
            pltpu.VMEM((nctx, GROUP, rows), F32),
            pltpu.VMEM((nctx, GROUP, rows), F32),
            pltpu.VMEM((nb, 2 * GROUP, 2 * block), F32),
            pltpu.VMEM((nb + 4, GROUP, 2 * block), F32),
            pltpu.VMEM((nb, 2 * GROUP, 2 * block), F32),
            pltpu.VMEM((nctx, 2 * GROUP, rows), F32),
            pltpu.SemaphoreType.REGULAR((3,)),
            dma((10,)),
            dma,
            dma((YN - 1, 2)),
            dma((2, YN, 2)),
            dma((YN, 2)),
        ]
        + [dma] * 6,
        compiler_params=pltpu.CompilerParams(
            collective_id=0, has_side_effects=True, vmem_limit_bytes=63 * 1024 * 1024
        ),
    )(
        filter_taps, k_proj, v_proj, q_proj, out_grad, out_weight,
        jnp.asarray(forward), jnp.asarray(back),
    )
    return pl.pallas_call(
        finish,
        out_shape=shapes,
        in_specs=[hbm] * 5,
        out_specs=(hbm,) * 4,
        scratch_shapes=[
            pltpu.VMEM((nctx, 2 * GROUP, rows), F32),
            pltpu.VMEM((chans, rows), F32),
        ]
        + [pltpu.VMEM((rows, chans), BF16)] * 6
        + [pltpu.VMEM((rows, chans), F32), dma((5,)), dma((4,))],
        compiler_params=pltpu.CompilerParams(vmem_limit_bytes=63 * 1024 * 1024),
    )(*results, saved_conv, k_proj, v_proj)


def solution(mesh):
    block = P("ctx", "tp")
    in_specs = (block, block, block, block, block, P("tp", None), block)
    return jax.shard_map(
        body, mesh=mesh, in_specs=in_specs, out_specs=(block,) * 4, check_vma=False
    )
```

```python
import functools
import math

import jax
import jax.numpy as jnp
import ml_dtypes
import numpy as np
from jax import lax
from jax.experimental import pallas as pl
from jax.experimental.pallas import tpu as pltpu
from jax.sharding import PartitionSpec as P

MESH = pl.DeviceIdType.MESH
F32 = jnp.float32
BF16 = jnp.bfloat16
XN = 4
YN = 4
GROUP = 8
DIRECT = (0, 3)


def halves(table):
    upper = table.astype(ml_dtypes.bfloat16)
    lower = (table - upper.astype(np.float64)).astype(ml_dtypes.bfloat16)
    return np.concatenate([upper, lower], axis=1)


def make_tables(block):
    n = np.arange(block)
    turns = np.outer(n, 2 * n + 1) % (4 * block)
    angle = turns * (math.pi / (2 * block))
    forward = np.concatenate([np.cos(angle), -np.sin(angle)], axis=1)
    back = np.concatenate([np.cos(angle).T, -np.sin(angle).T], axis=0) / block
    return halves(forward), halves(back)


def far_first(nctx):
    def hops(i):
        return min(i // 4, nctx // 4 - i // 4)

    return sorted(range(nctx), key=hops, reverse=True)


def split(value):
    upper = value.astype(BF16)
    return upper, (value - upper.astype(F32)).astype(BF16)


def mm(left, right):
    return jnp.dot(left, right, preferred_element_type=F32)


def fused(
    nctx, f_hbm, k_hbm, v_hbm, q_hbm, og_hbm, w_hbm, fwd_hbm, inv_hbm,
    ret, acc_hbm,
    f_ref, k_ref, v_ref, q_ref, og_ref, w, fwd, inv, og_all, acc, qt, fgs, xf, zs, zin, xspec, zt, obuf, rs,
    ready, local_sem, send_ag, recv_y, recv_x, recv_r, send_f, recv_f, send_z, recv_z, send_o, recv_o,
):
    rows, chans = q_ref.shape
    nb = nctx // 2
    block = 2 * rows
    half = rows // 2
    me_c = lax.axis_index("ctx")
    me_t = lax.axis_index("tp")
    x = lax.div(me_t, YN)
    y = lax.rem(me_t, YN)
    right = lax.rem(x + 1, XN)
    left = lax.rem(x + XN - 1, XN)
    across = lax.rem(x + 2, XN)
    line = [y, y + 1 - 2 * lax.rem(y, 2), lax.rem(y + 2, YN), YN - 1 - y]
    slot_me = lax.rem(me_c, 2) * nb + lax.div(me_c, 2)

    sources = (og_hbm, f_hbm, k_hbm, v_hbm, q_hbm, w_hbm, fwd_hbm, inv_hbm)
    targets = (og_ref, f_ref, k_ref, v_ref, q_ref, w, fwd, inv)
    loads = [
        pltpu.make_async_copy(source, target, local_sem.at[i])
        for i, (source, target) in enumerate(zip(sources, targets))
    ]
    for load in loads:
        load.start()

    barrier = pltpu.get_barrier_semaphore()

    def signal(c, t):
        pl.semaphore_signal(barrier, inc=1, device_id=(c, t), device_id_type=MESH)

    mate = x * YN + lax.rem(y + 2, YN)
    core = me_c + 1 - 2 * lax.rem(me_c, 2)
    turn = 2 - 4 * lax.rem(lax.div(me_c, 2), 2)

    def around(steps):
        return [lax.rem(me_c + i, nctx) for i in sorted({steps % nctx, -steps % nctx} - {0})]

    for t in (right, left, across):
        signal(me_c, t * YN + y)
    for j in range(1, YN):
        signal(me_c, x * YN + line[j])
    for c in (core, me_c + turn, core + turn):
        signal(c, mate)
    near = (*around(4), *around(8))
    for c in near:
        signal(c, me_t)

    def tell(partners, sem):
        for c in partners:
            pl.semaphore_signal(sem, inc=1, device_id=(c, me_t), device_id_type=MESH)

    loads[0].wait()
    pl.semaphore_wait(barrier, 6 + YN - 1 + len(near))
    tell(around(4), ready.at[0])

    def part(ref, h):
        return ref.at[pl.ds(h * half, half), :]

    def send(src, slot, h, dest_x, dest_y, sem):
        pltpu.make_async_remote_copy(
            src_ref=src,
            dst_ref=og_all.at[slot, pl.ds(h * half, half), :],
            send_sem=send_ag,
            recv_sem=sem,
            device_id=(me_c, dest_x * YN + dest_y),
            device_id_type=MESH,
        ).start()

    def arrived(slot, h, sem):
        dst = og_all.at[slot, pl.ds(h * half, half), :]
        pltpu.make_async_copy(dst, dst, sem).wait()

    def send_x(j, h):
        slot = x * YN + line[j]
        src = part(og_ref, h) if j == 0 else og_all.at[slot, pl.ds(h * half, half), :]
        if j in DIRECT:
            send(src, slot, h, across, y, recv_r.at[j, h])
        first, second = (right, left) if h == 0 else (left, right)
        send(src, slot, h, first, y, recv_x.at[h, j, h])
        send(src, slot, h, second, y, recv_x.at[1 - h, j, h])

    def relay(j):
        for h, source, dest in ((0, left, right), (1, right, left)):
            slot = source * YN + line[j]
            arrived(slot, h, recv_x.at[h, j, h])
            if j in DIRECT:
                continue
            send(og_all.at[slot, pl.ds(h * half, half), :], slot, h, dest, y, recv_r.at[j, h])

    def add(slot, block_value):
        cols = pl.ds(pl.multiple_of(slot * chans, chans), chans)
        acc[...] += lax.dot_general(
            w[:, cols], block_value, (((1,), (1,)), ((), ())), preferred_element_type=F32
        )

    def add_near(j):
        for way, source in ((0, left), (1, right)):
            slot = source * YN + line[j]
            arrived(slot, 1 - way, recv_x.at[way, j, 1 - way])
            add(slot, og_all[slot])

    def add_far(j):
        slot = across * YN + line[j]
        for h in range(2):
            arrived(slot, h, recv_r.at[j, h])
        add(slot, og_all[slot])

    def forward_line(j):
        slot = x * YN + line[j]
        for h in range(2):
            arrived(slot, h, recv_y.at[j - 1, h])
            send_x(j, h)

    for h in range(2):
        for j in range(1, YN):
            send(part(og_ref, h), me_t, h, x, line[j], recv_y.at[j - 1, h])
        send_x(0, h)

    def exchange(src, dst, send_sem, recv_sem):
        for i in far_first(nctx):
            peer = lax.rem(me_c + i, nctx)
            pltpu.make_async_remote_copy(
                src_ref=src(peer),
                dst_ref=dst,
                send_sem=send_sem,
                recv_sem=recv_sem,
                device_id=(peer, mate),
                device_id_type=MESH,
            ).start()

    def drain(ref, count, sem):
        whole = ref.at[pl.ds(0, count)]
        pltpu.make_async_copy(whole, whole, sem).wait()

    for load in loads[1:5]:
        load.wait()
    ft = f_ref[...].astype(F32).T.reshape(nctx, GROUP, rows)
    gated = (k_ref[...].astype(F32) * v_ref[...].astype(F32)).astype(BF16)
    gt = gated.astype(F32).T.reshape(nctx, GROUP, rows)
    fgs[...] = jnp.concatenate([ft, gt], axis=1).astype(BF16)
    qt[...] = q_ref[...].astype(F32).T

    for load in loads[5:]:
        load.wait()
    acc[...] = lax.dot_general(
        w[:, pl.ds(pl.multiple_of(me_t * chans, chans), chans)], og_ref[...],
        (((1,), (1,)), ((), ())), preferred_element_type=F32,
    )
    rounds = (around(4), around(12))
    for j in range(1, YN):
        forward_line(j)
        relay(j - 1)
        if j < 3:
            pl.semaphore_wait(ready.at[j - 1], len(rounds[j - 1]))
        if j == 1:
            tell(rounds[1], ready.at[1])
        if j == 3:
            exchange(lambda p: fgs.at[p], xf.at[slot_me], send_f, recv_f)
        slot = x * YN + line[j]
        add(slot, og_all[slot])
        add_near(j - 1)
        if j >= 2:
            add_far(j - 2)
    relay(YN - 1)
    add_near(YN - 1)
    add_far(YN - 2)
    add_far(YN - 1)

    zs[...] = (acc[...] * qt[...]).reshape(nctx, GROUP, rows)
    exchange(lambda p: zs.at[p], zin.at[slot_me], send_z, recv_z)

    save = pltpu.make_async_copy(acc, acc_hbm, local_sem.at[8])
    save.start()
    drain(xf, nctx, recv_f)
    taps = jnp.concatenate(
        [
            xf[pl.ds(0, nb)].reshape(nb * 2 * GROUP, rows),
            xf[pl.ds(nb, nb)].reshape(nb * 2 * GROUP, rows),
        ],
        axis=1,
    )
    both = mm(taps, fwd[...])
    xspec[...] = (both[:, : 2 * block] + both[:, 2 * block :]).reshape(nb, 2 * GROUP, 2 * block)
    lane = lax.broadcasted_iota(jnp.int32, (1, 1, block), 2)
    sign = (1 - 2 * lax.rem(lane, 2)).astype(F32)

    drain(zin, nctx, recv_z)
    signal_in = jnp.concatenate(
        [
            zin[pl.ds(0, nb)].reshape(nb * GROUP, rows),
            zin[pl.ds(nb, nb)].reshape(nb * GROUP, rows),
        ],
        axis=1,
    )
    upper, lower = split(signal_in)
    spec = mm(upper, fwd[...])
    spec = spec[:, : 2 * block] + spec[:, 2 * block :] + mm(lower, fwd[:, : 2 * block])
    spec = spec.reshape(nb, GROUP, 2 * block)
    real, imag = spec[:, :, :block], spec[:, :, block:]
    none = jnp.zeros((1, GROUP, block), F32)
    next_real = jnp.concatenate([real[1:], none], axis=0)
    next_imag = jnp.concatenate([imag[1:], none], axis=0)
    zt[pl.ds(0, nb), :, pl.ds(0, block)] = real + sign * next_imag
    zt[pl.ds(0, nb), :, pl.ds(block, block)] = imag - sign * next_real
    tile = min(4, nb)
    zt[pl.ds(nb, tile)] = jnp.zeros((tile, GROUP, 2 * block), F32)

    width = 128
    for part_of in range(block // width):
        re_cols = pl.ds(part_of * width, width)
        im_cols = pl.ds(block + part_of * width, width)
        for first in range(0, nb, tile):

            def steps(step, sums, re_cols=re_cols, im_cols=im_cols, first=first):
                sums = list(sums)
                for u in range(tile):
                    j = step * tile + u
                    taps_re = xspec[j, :, re_cols]
                    taps_im = xspec[j, :, im_cols]
                    for i in range(tile):
                        z_re = zt[j + first + i, :, re_cols]
                        z_im = zt[j + first + i, :, im_cols]
                        for kind in range(2):
                            a = taps_re[kind * GROUP : (kind + 1) * GROUP]
                            b = taps_im[kind * GROUP : (kind + 1) * GROUP]
                            at = (i * 2 + kind) * 2
                            sums[at] = sums[at] + (a * z_re + b * z_im)
                            sums[at + 1] = sums[at + 1] + (a * z_im - b * z_re)
                return tuple(sums)

            zero = jnp.zeros((GROUP, width), F32)
            sums = lax.fori_loop(0, (nb - first) // tile, steps, (zero,) * (4 * tile))
            for i in range(tile):
                for kind in range(2):
                    at = (i * 2 + kind) * 2
                    lines = pl.ds(kind * GROUP, GROUP)
                    obuf[first + i, lines, re_cols] = sums[at]
                    obuf[first + i, lines, im_cols] = sums[at + 1]

    upper, lower = split(obuf[...].reshape(nb * 2 * GROUP, 2 * block))
    both = mm(upper, inv[...])
    res = both[:, :block] + both[:, block:] + mm(lower, inv[:, :block])
    coded = (res * jnp.abs(res)).astype(BF16)
    rs[pl.ds(0, nb)] = coded[:, :rows].reshape(nb, 2 * GROUP, rows)
    rs[pl.ds(nb, nb)] = coded[:, rows:].reshape(nb, 2 * GROUP, rows)
    exchange(
        lambda p: rs.at[lax.rem(p, 2) * nb + lax.div(p, 2)], ret.at[me_c], send_o, recv_o
    )
    drain(ret, nctx, recv_o)
    save.wait()
    drain(og_all, XN * YN - 1, send_ag)
    drain(fgs, nctx, send_f)
    drain(zs, nctx, send_z)
    drain(rs, nctx, send_o)


def finish(
    ret_hbm, acc_hbm, s_hbm, k_hbm, v_hbm, dq_hbm, dk_hbm, dv_hbm, fg_hbm,
    ret, acc, s_ref, k_ref, v_ref, dq, dk, dv, fg, sem_in, sem_out,
):
    rows, chans = s_ref.shape
    loads = [
        pltpu.make_async_copy(source, target, sem_in.at[i])
        for i, (source, target) in enumerate(
            ((acc_hbm, acc), (s_hbm, s_ref), (ret_hbm, ret), (k_hbm, k_ref), (v_hbm, v_ref))
        )
    ]
    for load in loads:
        load.start()
    stores = [
        pltpu.make_async_copy(source, target, sem_out.at[i])
        for i, (source, target) in enumerate(
            ((dq, dq_hbm), (dk, dk_hbm), (dv, dv_hbm), (fg, fg_hbm))
        )
    ]
    loads[0].wait()
    loads[1].wait()
    dq[...] = (acc[...].T * s_ref[...].astype(F32)).astype(BF16)
    stores[0].start()
    loads[2].wait()
    coded = ret[...].astype(F32)
    root = jnp.sqrt(jnp.abs(coded))
    plain = jnp.where(coded < 0.0, -root, root)
    lagged = plain[:, GROUP:, :].reshape(chans, rows).T
    fg[...] = lagged * float(rows * ret.shape[0]) ** (-0.5)
    stores[3].start()
    du = plain[:, :GROUP, :].reshape(chans, rows).T
    loads[3].wait()
    loads[4].wait()
    dk[...] = (du * v_ref[...].astype(F32)).astype(BF16)
    stores[1].start()
    dv[...] = (du * k_ref[...].astype(F32)).astype(BF16)
    stores[2].start()
    for store in stores:
        store.wait()


def body(q_proj, k_proj, v_proj, saved_conv, out_grad, out_weight, filter_taps):
    rows, chans = q_proj.shape
    nctx = lax.axis_size("ctx")
    nb = nctx // 2
    block = 2 * rows
    forward, back = make_tables(block)
    hbm = pl.BlockSpec(memory_space=pltpu.HBM)
    dma = pltpu.SemaphoreType.DMA
    narrow = jax.ShapeDtypeStruct((rows, chans), BF16)
    shapes = (narrow, narrow, narrow, jax.ShapeDtypeStruct((rows, chans), F32))
    results = pl.pallas_call(
        functools.partial(fused, nctx),
        out_shape=(
            jax.ShapeDtypeStruct((nctx, 2 * GROUP, rows), BF16),
            jax.ShapeDtypeStruct((chans, rows), F32),
        ),
        in_specs=[hbm] * 8,
        out_specs=(hbm,) * 2,
        scratch_shapes=[pltpu.VMEM((rows, chans), BF16)] * 5
        + [
            pltpu.VMEM(out_weight.shape, BF16),
            pltpu.VMEM(forward.shape, BF16),
            pltpu.VMEM(back.shape, BF16),
            pltpu.VMEM((XN * YN, rows, chans), BF16),
            pltpu.VMEM((chans, rows), F32),
            pltpu.VMEM((chans, rows), F32),
            pltpu.VMEM((nctx, 2 * GROUP, rows), BF16),
            pltpu.VMEM((nctx, 2 * GROUP, rows), BF16),
            pltpu.VMEM((nctx, GROUP, rows), F32),
            pltpu.VMEM((nctx, GROUP, rows), F32),
            pltpu.VMEM((nb, 2 * GROUP, 2 * block), F32),
            pltpu.VMEM((nb + 4, GROUP, 2 * block), F32),
            pltpu.VMEM((nb, 2 * GROUP, 2 * block), F32),
            pltpu.VMEM((nctx, 2 * GROUP, rows), BF16),
            pltpu.SemaphoreType.REGULAR((2,)),
            dma((9,)),
            dma,
            dma((YN - 1, 2)),
            dma((2, YN, 2)),
            dma((YN, 2)),
        ]
        + [dma] * 6,
        compiler_params=pltpu.CompilerParams(
            collective_id=0, has_side_effects=True, vmem_limit_bytes=63 * 1024 * 1024
        ),
    )(
        filter_taps, k_proj, v_proj, q_proj, out_grad, out_weight,
        jnp.asarray(forward), jnp.asarray(back),
    )
    return pl.pallas_call(
        finish,
        out_shape=shapes,
        in_specs=[hbm] * 5,
        out_specs=(hbm,) * 4,
        scratch_shapes=[
            pltpu.VMEM((nctx, 2 * GROUP, rows), BF16),
            pltpu.VMEM((chans, rows), F32),
        ]
        + [pltpu.VMEM((rows, chans), BF16)] * 6
        + [pltpu.VMEM((rows, chans), F32), dma((5,)), dma((4,))],
        compiler_params=pltpu.CompilerParams(vmem_limit_bytes=63 * 1024 * 1024),
    )(*results, saved_conv, k_proj, v_proj)


def solution(mesh):
    block = P("ctx", "tp")
    in_specs = (block, block, block, block, block, P("tp", None), block)
    return jax.shard_map(
        body, mesh=mesh, in_specs=in_specs, out_specs=(block,) * 4, check_vma=False
    )
```

```python
import functools
import math

import jax
import jax.numpy as jnp
import ml_dtypes
import numpy as np
from jax import lax
from jax.experimental import pallas as pl
from jax.experimental.pallas import tpu as pltpu
from jax.sharding import PartitionSpec as P

MESH = pl.DeviceIdType.MESH
F32 = jnp.float32
BF16 = jnp.bfloat16
XN = 4
YN = 4
GROUP = 8
DIRECT = (0, 3)


def halves(table):
    upper = table.astype(ml_dtypes.bfloat16)
    lower = (table - upper.astype(np.float64)).astype(ml_dtypes.bfloat16)
    return np.concatenate([upper, lower], axis=1)


def make_tables(block):
    n = np.arange(block)
    turns = np.outer(n, 2 * n + 1) % (4 * block)
    angle = turns * (math.pi / (2 * block))
    forward = np.concatenate([np.cos(angle), -np.sin(angle)], axis=1)
    back = np.concatenate([np.cos(angle).T, -np.sin(angle).T], axis=0) / block
    return halves(forward), halves(back)


def planes(nctx):
    return nctx // 4


def ways_in(nctx):
    count = planes(nctx)

    def hops(one, other):
        return min((one - other) % count, (other - one) % count)

    return sorted(
        range(nctx), key=lambda c: hops(c // 4, count - 1) + hops(c // 4, 0), reverse=True
    )


def ways_out(nctx):
    count = planes(nctx)

    def entry(c):
        z = c // 4
        return z + (2 if 2 * z >= count else 0) + (4 if (c // 2) % 2 else 0)

    return sorted(range(nctx), key=entry)


def split(value):
    upper = value.astype(BF16)
    return upper, (value - upper.astype(F32)).astype(BF16)


def mm(left, right):
    return jnp.dot(left, right, preferred_element_type=F32)


def fused(
    nctx, f_hbm, k_hbm, v_hbm, q_hbm, og_hbm, w_hbm, fwd_hbm, inv_hbm,
    ret, acc_hbm,
    f_ref, k_ref, v_ref, q_ref, og_ref, w, fwd, inv, og_all, acc, qt, fgs, xf, zs, zin, xspec, zt, obuf, rs,
    ready, local_sem, send_ag, recv_y, recv_x, recv_r, send_f, recv_f, send_z, recv_z, send_o, recv_o,
):
    rows, chans = q_ref.shape
    nb = nctx // 2
    block = 2 * rows
    half = rows // 2
    me_c = lax.axis_index("ctx")
    me_t = lax.axis_index("tp")
    x = lax.div(me_t, YN)
    y = lax.rem(me_t, YN)
    right = lax.rem(x + 1, XN)
    left = lax.rem(x + XN - 1, XN)
    across = lax.rem(x + 2, XN)
    line = [y, y + 1 - 2 * lax.rem(y, 2), lax.rem(y + 2, YN), YN - 1 - y]
    slot_me = lax.rem(me_c, 2) * nb + lax.div(me_c, 2)

    sources = (og_hbm, f_hbm, k_hbm, v_hbm, q_hbm, w_hbm, fwd_hbm, inv_hbm)
    targets = (og_ref, f_ref, k_ref, v_ref, q_ref, w, fwd, inv)
    loads = [
        pltpu.make_async_copy(source, target, local_sem.at[i])
        for i, (source, target) in enumerate(zip(sources, targets))
    ]
    for load in loads:
        load.start()

    barrier = pltpu.get_barrier_semaphore()

    def signal(c, t):
        pl.semaphore_signal(barrier, inc=1, device_id=(c, t), device_id_type=MESH)

    mate = x * YN + lax.rem(y + 2, YN)
    core = me_c + 1 - 2 * lax.rem(me_c, 2)
    turn = 2 - 4 * lax.rem(lax.div(me_c, 2), 2)

    def around(steps):
        return [lax.rem(me_c + i, nctx) for i in sorted({steps % nctx, -steps % nctx} - {0})]

    for t in (right, left, across):
        signal(me_c, t * YN + y)
    for j in range(1, YN):
        signal(me_c, x * YN + line[j])
    for c in (core, me_c + turn, core + turn):
        signal(c, mate)
    near = (*around(4), *around(8))
    for c in near:
        signal(c, me_t)

    def tell(partners, sem):
        for c in partners:
            pl.semaphore_signal(sem, inc=1, device_id=(c, me_t), device_id_type=MESH)

    loads[0].wait()
    pl.semaphore_wait(barrier, 6 + YN - 1 + len(near))
    tell(around(4), ready.at[0])

    def part(ref, h):
        return ref.at[pl.ds(h * half, half), :]

    def send(src, slot, h, dest_x, dest_y, sem):
        pltpu.make_async_remote_copy(
            src_ref=src,
            dst_ref=og_all.at[slot, pl.ds(h * half, half), :],
            send_sem=send_ag,
            recv_sem=sem,
            device_id=(me_c, dest_x * YN + dest_y),
            device_id_type=MESH,
        ).start()

    def arrived(slot, h, sem):
        dst = og_all.at[slot, pl.ds(h * half, half), :]
        pltpu.make_async_copy(dst, dst, sem).wait()

    def send_x(j, h):
        slot = x * YN + line[j]
        src = part(og_ref, h) if j == 0 else og_all.at[slot, pl.ds(h * half, half), :]
        if j in DIRECT:
            send(src, slot, h, across, y, recv_r.at[j, h])
        first, second = (right, left) if h == 0 else (left, right)
        send(src, slot, h, first, y, recv_x.at[h, j, h])
        send(src, slot, h, second, y, recv_x.at[1 - h, j, h])

    def relay(j):
        for h, source, dest in ((0, left, right), (1, right, left)):
            slot = source * YN + line[j]
            arrived(slot, h, recv_x.at[h, j, h])
            if j in DIRECT:
                continue
            send(og_all.at[slot, pl.ds(h * half, half), :], slot, h, dest, y, recv_r.at[j, h])

    def add(slot, block_value):
        cols = pl.ds(pl.multiple_of(slot * chans, chans), chans)
        acc[...] += lax.dot_general(
            w[:, cols], block_value, (((1,), (1,)), ((), ())), preferred_element_type=F32
        )

    def add_near(j):
        for way, source in ((0, left), (1, right)):
            slot = source * YN + line[j]
            arrived(slot, 1 - way, recv_x.at[way, j, 1 - way])
            add(slot, og_all[slot])

    def add_far(j):
        slot = across * YN + line[j]
        for h in range(2):
            arrived(slot, h, recv_r.at[j, h])
        add(slot, og_all[slot])

    def forward_line(j):
        slot = x * YN + line[j]
        for h in range(2):
            arrived(slot, h, recv_y.at[j - 1, h])
            send_x(j, h)

    for j in range(1, YN):
        for h in range(2):
            send(part(og_ref, h), me_t, h, x, line[j], recv_y.at[j - 1, h])
    for h in range(2):
        send_x(0, h)

    def exchange(order, src, dst, send_sem, recv_sem):
        for peer in order:
            pltpu.make_async_remote_copy(
                src_ref=src(peer),
                dst_ref=dst,
                send_sem=send_sem,
                recv_sem=recv_sem,
                device_id=(peer, mate),
                device_id_type=MESH,
            ).start()

    def drain(ref, count, sem):
        whole = ref.at[pl.ds(0, count)]
        pltpu.make_async_copy(whole, whole, sem).wait()

    for load in loads[1:5]:
        load.wait()
    ft = f_ref[...].astype(F32).T.reshape(nctx, GROUP, rows)
    gated = (k_ref[...].astype(F32) * v_ref[...].astype(F32)).astype(BF16)
    gt = gated.astype(F32).T.reshape(nctx, GROUP, rows)
    fgs[...] = jnp.concatenate([ft, gt], axis=1).astype(BF16)
    qt[...] = q_ref[...].astype(F32).T

    for load in loads[5:]:
        load.wait()
    acc[...] = lax.dot_general(
        w[:, pl.ds(pl.multiple_of(me_t * chans, chans), chans)], og_ref[...],
        (((1,), (1,)), ((), ())), preferred_element_type=F32,
    )
    rounds = (around(4), around(12))
    pl.semaphore_wait(ready.at[0], len(rounds[0]))
    tell(rounds[1], ready.at[1])
    for j in range(1, YN):
        forward_line(j)
        relay(j - 1)
        if j == 2:
            pl.semaphore_wait(ready.at[1], len(rounds[1]))
            exchange(ways_in(nctx), lambda p: fgs.at[p], xf.at[slot_me], send_f, recv_f)
        slot = x * YN + line[j]
        add(slot, og_all[slot])
        add_near(j - 1)
        if j >= 2:
            add_far(j - 2)
    relay(YN - 1)
    add_near(YN - 1)
    add_far(YN - 2)
    add_far(YN - 1)

    zs[...] = (acc[...] * qt[...]).reshape(nctx, GROUP, rows)
    exchange(ways_in(nctx), lambda p: zs.at[p], zin.at[slot_me], send_z, recv_z)

    save = pltpu.make_async_copy(acc, acc_hbm, local_sem.at[8])
    save.start()
    drain(xf, nctx, recv_f)
    taps = jnp.concatenate(
        [
            xf[pl.ds(0, nb)].reshape(nb * 2 * GROUP, rows),
            xf[pl.ds(nb, nb)].reshape(nb * 2 * GROUP, rows),
        ],
        axis=1,
    )
    both = mm(taps, fwd[...])
    xspec[...] = (both[:, : 2 * block] + both[:, 2 * block :]).reshape(nb, 2 * GROUP, 2 * block)
    lane = lax.broadcasted_iota(jnp.int32, (1, 1, block), 2)
    sign = (1 - 2 * lax.rem(lane, 2)).astype(F32)

    drain(zin, nctx, recv_z)
    signal_in = jnp.concatenate(
        [
            zin[pl.ds(0, nb)].reshape(nb * GROUP, rows),
            zin[pl.ds(nb, nb)].reshape(nb * GROUP, rows),
        ],
        axis=1,
    )
    upper, lower = split(signal_in)
    spec = mm(upper, fwd[...])
    spec = spec[:, : 2 * block] + spec[:, 2 * block :] + mm(lower, fwd[:, : 2 * block])
    spec = spec.reshape(nb, GROUP, 2 * block)
    real, imag = spec[:, :, :block], spec[:, :, block:]
    none = jnp.zeros((1, GROUP, block), F32)
    next_real = jnp.concatenate([real[1:], none], axis=0)
    next_imag = jnp.concatenate([imag[1:], none], axis=0)
    zt[pl.ds(0, nb), :, pl.ds(0, block)] = real + sign * next_imag
    zt[pl.ds(0, nb), :, pl.ds(block, block)] = imag - sign * next_real
    tile = min(4, nb)
    zt[pl.ds(nb, tile)] = jnp.zeros((tile, GROUP, 2 * block), F32)

    width = 128
    for first in range(0, nb, tile):
        for part_of in range(block // width):
            re_cols = pl.ds(part_of * width, width)
            im_cols = pl.ds(block + part_of * width, width)

            def steps(step, sums, re_cols=re_cols, im_cols=im_cols, first=first):
                sums = list(sums)
                for u in range(tile):
                    j = step * tile + u
                    taps_re = xspec[j, :, re_cols]
                    taps_im = xspec[j, :, im_cols]
                    for i in range(tile):
                        z_re = zt[j + first + i, :, re_cols]
                        z_im = zt[j + first + i, :, im_cols]
                        for kind in range(2):
                            a = taps_re[kind * GROUP : (kind + 1) * GROUP]
                            b = taps_im[kind * GROUP : (kind + 1) * GROUP]
                            at = (i * 2 + kind) * 2
                            sums[at] = sums[at] + (a * z_re + b * z_im)
                            sums[at + 1] = sums[at + 1] + (a * z_im - b * z_re)
                return tuple(sums)

            zero = jnp.zeros((GROUP, width), F32)
            sums = lax.fori_loop(0, (nb - first) // tile, steps, (zero,) * (4 * tile))
            for i in range(tile):
                for kind in range(2):
                    at = (i * 2 + kind) * 2
                    lines = pl.ds(kind * GROUP, GROUP)
                    obuf[first + i, lines, re_cols] = sums[at]
                    obuf[first + i, lines, im_cols] = sums[at + 1]
        upper, lower = split(obuf[pl.ds(first, tile)].reshape(tile * 2 * GROUP, 2 * block))
        both = mm(upper, inv[...])
        res = both[:, :block] + both[:, block:] + mm(lower, inv[:, :block])
        coded = (res * jnp.abs(res)).astype(BF16)
        rs[pl.ds(first, tile)] = coded[:, :rows].reshape(tile, 2 * GROUP, rows)
        rs[pl.ds(nb + first, tile)] = coded[:, rows:].reshape(tile, 2 * GROUP, rows)
        exchange(
            [c for c in ways_out(nctx) if first <= c // 2 < first + tile],
            lambda p: rs.at[p % 2 * nb + p // 2], ret.at[me_c], send_o, recv_o,
        )

    drain(ret, nctx, recv_o)
    save.wait()
    drain(og_all, XN * YN - 1, send_ag)
    drain(fgs, nctx, send_f)
    drain(zs, nctx, send_z)
    drain(rs, nctx, send_o)


def finish(
    ret_hbm, acc_hbm, s_hbm, k_hbm, v_hbm, dq_hbm, dk_hbm, dv_hbm, fg_hbm,
    ret, acc, s_ref, k_ref, v_ref, dq, dk, dv, fg, sem_in, sem_out,
):
    rows, chans = s_ref.shape
    loads = [
        pltpu.make_async_copy(source, target, sem_in.at[i])
        for i, (source, target) in enumerate(
            ((acc_hbm, acc), (s_hbm, s_ref), (ret_hbm, ret), (k_hbm, k_ref), (v_hbm, v_ref))
        )
    ]
    for load in loads:
        load.start()
    stores = [
        pltpu.make_async_copy(source, target, sem_out.at[i])
        for i, (source, target) in enumerate(
            ((dq, dq_hbm), (dk, dk_hbm), (dv, dv_hbm), (fg, fg_hbm))
        )
    ]
    loads[0].wait()
    loads[1].wait()
    dq[...] = (acc[...].T * s_ref[...].astype(F32)).astype(BF16)
    stores[0].start()
    loads[2].wait()
    coded = ret[...].astype(F32)
    root = jnp.sqrt(jnp.abs(coded))
    plain = jnp.where(coded < 0.0, -root, root)
    lagged = plain[:, GROUP:, :].reshape(chans, rows).T
    fg[...] = lagged * float(rows * ret.shape[0]) ** (-0.5)
    stores[3].start()
    du = plain[:, :GROUP, :].reshape(chans, rows).T
    loads[3].wait()
    loads[4].wait()
    dk[...] = (du * v_ref[...].astype(F32)).astype(BF16)
    stores[1].start()
    dv[...] = (du * k_ref[...].astype(F32)).astype(BF16)
    stores[2].start()
    for store in stores:
        store.wait()


def body(q_proj, k_proj, v_proj, saved_conv, out_grad, out_weight, filter_taps):
    rows, chans = q_proj.shape
    nctx = lax.axis_size("ctx")
    nb = nctx // 2
    block = 2 * rows
    forward, back = make_tables(block)
    hbm = pl.BlockSpec(memory_space=pltpu.HBM)
    dma = pltpu.SemaphoreType.DMA
    narrow = jax.ShapeDtypeStruct((rows, chans), BF16)
    shapes = (narrow, narrow, narrow, jax.ShapeDtypeStruct((rows, chans), F32))
    results = pl.pallas_call(
        functools.partial(fused, nctx),
        out_shape=(
            jax.ShapeDtypeStruct((nctx, 2 * GROUP, rows), BF16),
            jax.ShapeDtypeStruct((chans, rows), F32),
        ),
        in_specs=[hbm] * 8,
        out_specs=(hbm,) * 2,
        scratch_shapes=[pltpu.VMEM((rows, chans), BF16)] * 5
        + [
            pltpu.VMEM(out_weight.shape, BF16),
            pltpu.VMEM(forward.shape, BF16),
            pltpu.VMEM(back.shape, BF16),
            pltpu.VMEM((XN * YN, rows, chans), BF16),
            pltpu.VMEM((chans, rows), F32),
            pltpu.VMEM((chans, rows), F32),
            pltpu.VMEM((nctx, 2 * GROUP, rows), BF16),
            pltpu.VMEM((nctx, 2 * GROUP, rows), BF16),
            pltpu.VMEM((nctx, GROUP, rows), F32),
            pltpu.VMEM((nctx, GROUP, rows), F32),
            pltpu.VMEM((nb, 2 * GROUP, 2 * block), F32),
            pltpu.VMEM((nb + 4, GROUP, 2 * block), F32),
            pltpu.VMEM((nb, 2 * GROUP, 2 * block), F32),
            pltpu.VMEM((nctx, 2 * GROUP, rows), BF16),
            pltpu.SemaphoreType.REGULAR((2,)),
            dma((9,)),
            dma,
            dma((YN - 1, 2)),
            dma((2, YN, 2)),
            dma((YN, 2)),
        ]
        + [dma] * 6,
        compiler_params=pltpu.CompilerParams(
            collective_id=0, has_side_effects=True, vmem_limit_bytes=63 * 1024 * 1024
        ),
    )(
        filter_taps, k_proj, v_proj, q_proj, out_grad, out_weight,
        jnp.asarray(forward), jnp.asarray(back),
    )
    return pl.pallas_call(
        finish,
        out_shape=shapes,
        in_specs=[hbm] * 5,
        out_specs=(hbm,) * 4,
        scratch_shapes=[
            pltpu.VMEM((nctx, 2 * GROUP, rows), BF16),
            pltpu.VMEM((chans, rows), F32),
        ]
        + [pltpu.VMEM((rows, chans), BF16)] * 6
        + [pltpu.VMEM((rows, chans), F32), dma((5,)), dma((4,))],
        compiler_params=pltpu.CompilerParams(vmem_limit_bytes=63 * 1024 * 1024),
    )(*results, saved_conv, k_proj, v_proj)


def solution(mesh):
    block = P("ctx", "tp")
    in_specs = (block, block, block, block, block, P("tp", None), block)
    return jax.shard_map(
        body, mesh=mesh, in_specs=in_specs, out_specs=(block,) * 4, check_vma=False
    )
```
